128 devices in a mesh: pipe: 2 (over y_hi), seq: 16 (over x, z), dp: 4 (over y_lo, core).
Axes of the slice: x: 4, y: 4 (y_hi: 2, y_lo: 2; y = y_hi * 2 + y_lo), z: 4, core: 2. Of those that a mesh axis runs over, the one named last changes fastest.
Arguments:
- queries: bfloat16 [2, 4, 16, 384, 1536], P('pipe', 'dp', 'seq'), may hold values from -18 to 18
- keys: bfloat16 [2, 4, 16, 384, 1536], P('pipe', 'dp', 'seq'), may hold values from -18 to 18
- values: bfloat16 [2, 4, 16, 384, 1536], P('pipe', 'dp', 'seq'), may hold values from -6 to 6
- grad_out: bfloat16 [2, 4, 16, 384, 1536], P('pipe', 'dp', 'seq'), may hold values from -20 to 20
- norm_gains: float32 [2, 2, 128], P('pipe'), may hold values from 0.5 to 1.5
- kv_tiles: int32 [2, 4, 16, 3], P('pipe', 'dp', 'seq'), may hold values from -1 to 15, as said below
Outputs:
- qkv_grad: bfloat16 [2, 3, 4, 16, 384, 1536], P('pipe', None, 'dp', 'seq')
- gain_grads: float32 [2, 2, 128], P('pipe')
The draws below stay inside these ranges and needn't reach their ends.
Inputs may be any that keep to these rules, and one draw needn't show every extreme that they name: `kv_tiles`: tile t covers frame tile t // 1 and spatial tile t % 1. The row of tile t names tile t itself and some of the other tiles of frame tiles t - 1, t // 1 and t + 1 inside the sample, each at most once, in some order; its other entries are -1.
All inputs are finite; a program needn't handle non-finite values.
Results may differ from the reference program's by a relative error of at most 0.007.
Values may be sent and summed in bfloat16 or wider, within the bound.
A program may use at most 256 MiB of HBM per device.

```python
import math
import jax
import jax.numpy as jnp
from jax import lax

TPD = 1
TILE = 384
HEADS = 12
HEAD_DIM = 128
SLOTS = 3
HD = 1536
FRAME_TILES = 16
TILES = 16
BATCH = 4
SEGMENTS = 2


def draw_kv_tiles(key, part):
    tile_ids = jnp.arange(TILES, dtype=jnp.int32)
    frame_ids = tile_ids // TPD
    slot_ids = jnp.arange(SLOTS, dtype=jnp.int32)
    frame_step = slot_ids // TPD - 1
    spot_ids = slot_ids % TPD
    cand_frame = frame_ids[:, None] + frame_step[None, :]
    usable = (cand_frame >= 0) & (cand_frame < FRAME_TILES)
    cand_tile = jnp.where(usable, cand_frame * TPD + spot_ids[None, :], -1)
    cand_full = jnp.broadcast_to(cand_tile, (SEGMENTS, BATCH, TILES, SLOTS))
    own_slot = cand_full == tile_ids[None, None, :, None]
    keep_bits = jax.random.randint(jax.random.fold_in(key, 5), (SEGMENTS, BATCH, TILES, SLOTS), 0, 2)
    kept = own_slot | (keep_bits == 1)
    cand_full = jnp.where(kept, cand_full, -1)
    random_rank = jax.random.randint(jax.random.fold_in(key, 7), (SEGMENTS, BATCH, TILES, SLOTS), 0, 1 << 20)
    ranking = random_rank * 64 + slot_ids
    order = jnp.argsort(ranking, axis=-1, stable=True)
    return jnp.take_along_axis(cand_full, order, axis=-1).astype(jnp.int32)


def token_scales(key, lowest, highest):
    full_shape = (SEGMENTS, BATCH, TILES, TILE, HEADS, 1)
    return jnp.exp(jax.random.uniform(key, full_shape, jnp.float32, jnp.log(lowest), jnp.log(highest)))


def headed(key):
    noise_key = jax.random.fold_in(key, 1)
    scale_key = jax.random.fold_in(key, 2)
    full_shape = (SEGMENTS, BATCH, TILES, TILE, HEADS, HEAD_DIM)
    noise_part = jnp.clip(jax.random.normal(noise_key, full_shape, jnp.float32), -4.0, 4.0)
    noise_part = noise_part * token_scales(scale_key, 0.3, 3.0)
    return noise_part.reshape(SEGMENTS, BATCH, TILES, TILE, HEADS * HEAD_DIM)


def draw_queries(key, part):
    return headed(jax.random.fold_in(key, 11)).astype(jnp.bfloat16)


def draw_keys(key, part):
    return headed(jax.random.fold_in(key, 23)).astype(jnp.bfloat16)


def draw_grad_out(key, part):
    noise_key = jax.random.fold_in(key, 31)
    full_shape = (SEGMENTS, BATCH, TILES, TILE, HEADS * HEAD_DIM)
    frame_pos = (jnp.arange(TILES, dtype=jnp.int32) // TPD).astype(jnp.float32)
    frame_ramp = (1.0 + 2.0 * frame_pos / (FRAME_TILES - 1)).reshape(1, 1, TILES, 1, 1)
    noise_part = jnp.clip(jax.random.normal(noise_key, full_shape, jnp.float32), -4.0, 4.0)
    return (noise_part * frame_ramp).astype(jnp.bfloat16)


def block_scale(rng, shape, split, least, high):
    gain, own = 1.0, jax.random.fold_in(rng, 6)
    for position, parts in split:
        steps = jnp.exp(jax.random.uniform(jax.random.fold_in(own, position), (parts,), jnp.float32, least / len(split), high / len(split)))
        gain = gain * jnp.repeat(steps, shape[position] // parts).reshape([-1 if axis == position else 1 for axis in range(len(shape))])
    return gain


def noise(own_key, shape, deviation, reach, pieces=(), kind=jnp.bfloat16):
    result = deviation * jax.random.normal(own_key, shape, jnp.float32)
    if pieces:
        result = result * block_scale(own_key, shape, pieces, -0.22, 0.18)
    return jnp.clip(result, -reach, reach).astype(kind)


def setup_inputs(seed: int = 0) -> dict:
    key_list = jax.random.split(jax.random.key(seed), 7)
    queries = draw_queries(jax.random.fold_in(key_list[6], 71), 0)
    keys = draw_keys(jax.random.fold_in(key_list[6], 71), 0)
    values = noise(key_list[2], (SEGMENTS, BATCH, TILES, TILE, HD), 1.0, 6.0, ((0, 2), (1, 4), (2, 16)))
    grad_out = draw_grad_out(jax.random.fold_in(key_list[6], 71), 0)
    norm_gains = jnp.clip(1.0 + 0.1 * jax.random.normal(key_list[4], (SEGMENTS, 2, HEAD_DIM), jnp.float32), 0.5, 1.5)
    kv_tiles = draw_kv_tiles(jax.random.fold_in(key_list[6], 71), 0)
    return dict(queries=queries, keys=keys, values=values, grad_out=grad_out, norm_gains=norm_gains, kv_tiles=kv_tiles)


epsilon = 1e-06

def normalize(source, gain_row):
    floats = source.astype(jnp.float32).reshape(source.shape[:-1] + (HEADS, HEAD_DIM))
    scaled = lax.rsqrt(lax.optimization_barrier(jnp.mean(floats * floats, axis=-1, keepdims=True)) + epsilon)
    normed = (floats * scaled * gain_row).astype(jnp.bfloat16)
    return (normed, floats, scaled)

def norm_back(grad_hat, floats, scaled, gain_row):
    projected = lax.optimization_barrier(jnp.sum(gain_row * grad_hat * floats, axis=-1, keepdims=True))
    gradient = scaled * gain_row * grad_hat - scaled ** 3 * floats * projected / HEAD_DIM
    gain_part = lax.optimization_barrier(jnp.sum((grad_hat * floats * scaled).reshape(-1, HEAD_DIM), axis=0))
    return (gradient.reshape(gradient.shape[:-2] + (HEADS * HEAD_DIM,)), gain_part)

def rounded(source):
    return lax.optimization_barrier(source.astype(jnp.bfloat16)).astype(jnp.float32)

def one_sample(query_in, key_in, value_in, grad_in, gain_rows, tile_lists):
    query_hat, query_floats, query_scale = normalize(query_in, gain_rows[0])
    key_hat, key_floats, key_scale = normalize(key_in, gain_rows[1])
    value_head = value_in.astype(jnp.float32).reshape(TILES, TILE, HEADS, HEAD_DIM)
    grad_head = grad_in.astype(jnp.float32).reshape(TILES, TILE, HEADS, HEAD_DIM)
    root_scale = HEAD_DIM ** (-0.5)

    def visit(carry, tile_index):
        key_acc, value_acc = carry
        listed = tile_lists[tile_index].astype(jnp.int32)
        live = (listed >= 0).astype(jnp.float32)
        chosen = jnp.maximum(listed, 0).astype(jnp.int32)
        key_mask = jnp.repeat(live, TILE)
        keys_here = key_hat[chosen].astype(jnp.float32).reshape(SLOTS * TILE, HEADS, HEAD_DIM)
        values_here = value_head[chosen].reshape(SLOTS * TILE, HEADS, HEAD_DIM)
        query_tile = query_hat[tile_index].astype(jnp.float32)
        grad_tile = grad_head[tile_index]
        scores = jnp.einsum('qhd,khd->hqk', query_tile, keys_here) * root_scale
        exp_scores = jnp.exp(scores) * key_mask
        attention = exp_scores / lax.optimization_barrier(jnp.sum(exp_scores, axis=-1, keepdims=True))
        grad_attn = jnp.einsum('qhd,khd->hqk', grad_tile, values_here)
        deltas = lax.optimization_barrier(jnp.sum(attention * grad_attn, axis=-1, keepdims=True))
        dscore = rounded(attention * (grad_attn - deltas))
        attn_low = rounded(attention)
        query_grad = jnp.einsum('hqk,khd->qhd', dscore, keys_here) * root_scale
        key_part = jnp.einsum('hqk,qhd->khd', dscore, query_tile) * root_scale
        value_part = jnp.einsum('hqk,qhd->khd', attn_low, grad_tile)
        slot_mask = live[:, None, None, None]
        key_acc = key_acc.at[chosen].add(key_part.reshape(SLOTS, TILE, HEADS, HEAD_DIM) * slot_mask)
        value_acc = value_acc.at[chosen].add(value_part.reshape(SLOTS, TILE, HEADS, HEAD_DIM) * slot_mask)
        return ((key_acc, value_acc), query_grad)
    zero_acc = jnp.zeros((TILES, TILE, HEADS, HEAD_DIM), jnp.float32)
    (key_acc, value_acc), query_grads = lax.scan(visit, (zero_acc, zero_acc), jnp.arange(TILES, dtype=jnp.int32))
    query_grad, query_gain = norm_back(query_grads, query_floats, query_scale, gain_rows[0])
    key_grad, key_gain = norm_back(key_acc, key_floats, key_scale, gain_rows[1])
    value_grad = value_acc.reshape(TILES, TILE, HEADS * HEAD_DIM)
    stacked = jnp.stack([query_grad, key_grad, value_grad]).astype(jnp.bfloat16)
    return (stacked, jnp.stack([query_gain, key_gain]))

def reference(queries, keys, values, grad_out, norm_gains, kv_tiles):
    segment_grads = []
    segment_gains = []
    for segment_index in range(SEGMENTS):
        sample_grads = []
        gain_total = jnp.zeros((2, HEAD_DIM), jnp.float32)
        for sample_index in range(BATCH):
            grads, gain_terms = one_sample(queries[segment_index, sample_index], keys[segment_index, sample_index], values[segment_index, sample_index], grad_out[segment_index, sample_index], norm_gains[segment_index], kv_tiles[segment_index, sample_index])
            sample_grads.append(grads)
            gain_total = gain_total + gain_terms
        segment_grads.append(jnp.stack(sample_grads, axis=1))
        segment_gains.append(gain_total / math.sqrt(BATCH * TILES * TILE * HEADS))
    grads_all = jnp.stack(segment_grads)
    return (jnp.roll(grads_all, -1, axis=0), jnp.stack(segment_gains))
```

```python
import math

import jax
import jax.numpy as jnp
from jax import lax
from jax.experimental import pallas as pl
from jax.experimental.pallas import tpu as pltpu
from jax.sharding import PartitionSpec as P

HEADS = 12
DIM = 128
TILE = 384
SPAN = 3 * TILE
EPSILON = 1e-06
SCALE = DIM**-0.5
EXP2_SCALE = SCALE * math.log2(math.e)
MESH = pl.DeviceIdType.MESH
BF16, F32 = jnp.bfloat16, jnp.float32

TOTAL_LAG, GRAD_LAG, QUERY_LAG, AHEAD = 1, 2, 4, 2
SLOTS = GRAD_LAG + 1
STEPS = HEADS + QUERY_LAG


def over_rows(a, b):
    return lax.dot_general(a, b, (((1,), (1,)), ((), ())), preferred_element_type=F32)


def product(a, b):
    return lax.dot_general(a, b, (((1,), (0,)), ((), ())), preferred_element_type=F32)


def inverse_norm(x):
    return lax.rsqrt(jnp.mean(x * x, axis=-1, keepdims=True) + EPSILON)


def norm_back(grad_hat, x, gain):
    inverse = inverse_norm(x)
    scaled = grad_hat * x
    projected = jnp.sum(gain * scaled, axis=-1, keepdims=True)
    grad = inverse * (gain * grad_hat) - x * (inverse * inverse * inverse * projected * (1.0 / DIM))
    return grad, jnp.sum(scaled * inverse, axis=0, keepdims=True)


def kernel(
    seqs, dps, zs,
    q_ref, k_ref, v_ref, g_ref, gain_ref, list_ref,
    out_ref, gain_out,
    q_raw, k_raw, v_in, pair, k_hat, k_turned, exps, gprobs, low, stat_own, stat_out, stat_in,
    tot_own, tot_out, tot_in, dq_own, dq_out, dq_in, results, gain_acc, gain_slots,
    load_sem, in_send, in_recv, stat_send, stat_recv, tot_send, tot_recv, dq_send, dq_recv,
    out_send, out_recv, gain_send, gain_recv,
):
    p, s, d = lax.axis_index("pipe"), lax.axis_index("seq"), lax.axis_index("dp")
    left, right = (p, lax.rem(s + seqs - 1, seqs), d), (p, lax.rem(s + 1, seqs), d)
    sides = (left, right)
    across = (1 - p, s, d)
    xs = seqs // zs
    x, z = s // zs, lax.rem(s, zs)
    groups = (
        (d, dps, lambda i: (p, s, i)),
        (x, xs, lambda i: (p, i * zs + z, d)),
        (z, zs, lambda i: (p, x * zs + i, d)),
    )

    def load(part, source, target, h):
        columns = pl.ds(pl.multiple_of(h * DIM, DIM), DIM)
        return pltpu.make_async_copy(source.at[:, columns], target, load_sem.at[part, h])

    def loads(h):
        return (
            load(0, q_ref, q_raw.at[h], h),
            load(1, k_ref, k_raw.at[h], h),
            load(2, g_ref, pair.at[h, 1, pl.ds(TILE, TILE)], h),
            load(3, v_ref, v_in.at[h], h),
        )

    def start_loads(h, carry):
        for copy in loads(h):
            copy.start()
        return carry

    lax.fori_loop(0, HEADS, start_loads, 0)

    barrier = pltpu.get_barrier_semaphore()
    greeted = [left, right, across]
    for mine, size, device in groups:
        greeted += [device(lax.rem(mine + j, size)) for j in range(1, size)]
    for device in greeted:
        pl.semaphore_signal(barrier, inc=1, device_id=device, device_id_type=MESH)

    def remote(source, target, send, recv, device):
        return pltpu.make_async_remote_copy(
            src_ref=source, dst_ref=target, send_sem=send, recv_sem=recv,
            device_id=device, device_id_type=MESH,
        )

    def send_pair(h, side):
        return remote(
            pair.at[h, :, pl.ds(TILE, TILE)], pair.at[h, :, pl.ds(2 * TILE * (1 - side), TILE)],
            in_send.at[h, side], in_recv.at[h, 1 - side], sides[side],
        )

    def send_block(out, into, send, recv):
        def copy(h, side):
            return remote(
                out.at[h, side], into.at[h, 1 - side], send.at[h, side], recv.at[h, 1 - side], sides[side]
            )
        return copy

    def take(copy, h):
        for side in (0, 1):
            copy(h, side).wait_recv()

    send_stat = send_block(stat_out, stat_in, stat_send, stat_recv)
    send_total = send_block(tot_out, tot_in, tot_send, tot_recv)
    send_dq = send_block(dq_out, dq_in, dq_send, dq_recv)

    def send_result(part, h):
        columns = pl.ds(pl.multiple_of(h * DIM, DIM), DIM)
        return remote(
            results.at[part, h], out_ref.at[part, :, columns],
            out_send.at[part, h], out_recv.at[part, h], across,
        )

    gains = [gain_ref[i : i + 1, :] for i in (0, 1)]

    def names(tile):
        named = (list_ref[0, 0] == tile) | (list_ref[0, 1] == tile) | (list_ref[0, 2] == tile)
        return jnp.where(named, 1.0, 0.0).astype(F32)

    masks = (jnp.where(s > 0, names(s - 1), 0.0), names(s + 1))

    def normalize(h):
        for copy in loads(h):
            copy.wait()
        q = q_raw[h].astype(F32)
        pair[h, 0, TILE : 2 * TILE] = (q * inverse_norm(q) * gains[0]).astype(BF16)

    def normalize_key(h):
        k = k_raw[h].astype(F32)
        hat = k * inverse_norm(k) * gains[1]
        k_hat[h] = hat.astype(BF16)
        k_turned[h] = hat.T.astype(BF16)

    def give_pair(h):
        for side in (0, 1):
            send_pair(h, side).start()

    def scores(h):
        slot = lax.rem(h, SLOTS)
        for b in range(3):
            span = slice(b * TILE, (b + 1) * TILE)
            e = jnp.exp2(over_rows(k_hat[h], pair[h, 0, span]) * EXP2_SCALE)
            g = over_rows(v_in[h], pair[h, 1, span])
            exps[slot, :, span] = e
            gprobs[slot, :, span] = g
            total = jnp.sum(e, axis=0, keepdims=True)
            delta = jnp.sum(e * g, axis=0, keepdims=True)
            target = stat_own.at[h] if b == 1 else stat_out.at[h, b // 2]
            target[0:1] = total
            target[1:2] = delta
        for side in (0, 1):
            send_stat(h, side).start()

    def totals(h):
        take(send_stat, h)
        both = stat_own[h] + masks[0] * stat_in[h, 0] + masks[1] * stat_in[h, 1]
        inverse = 1.0 / both[0:1]
        delta = both[1:2] * inverse
        tot_own[h, 0:1] = inverse
        tot_own[h, 1:2] = delta
        for side in (0, 1):
            tot_out[h, side, 0:1] = inverse * masks[side]
            tot_out[h, side, 1:2] = delta
            send_total(h, side).start()

    def grads(h):
        take(send_total, h)
        slot = lax.rem(h, SLOTS)
        for b in range(3):
            span = slice(b * TILE, (b + 1) * TILE)
            row = tot_own.at[h] if b == 1 else tot_in.at[h, b // 2]
            probs = exps[slot, :, span] * row[0:1]
            low[0, :, span] = probs.astype(BF16)
            low[1, :, span] = (probs * (gprobs[slot, :, span] - row[1:2])).astype(BF16)
        turned = product(k_turned[h], low[1])
        dq_out[h, 0] = turned[:, :TILE].astype(BF16)
        dq_out[h, 1] = turned[:, 2 * TILE :].astype(BF16)
        dq_own[h] = turned[:, TILE : 2 * TILE]
        for side in (0, 1):
            send_dq(h, side).start()
        results[2, h] = product(low[0], pair[h, 1]).astype(BF16)
        send_result(2, h).start()
        key_hat_grad = product(low[1], pair[h, 0]) * SCALE
        grad, gain = norm_back(key_hat_grad, k_raw[h].astype(F32), gains[1])
        gain_acc[1:2] += gain
        results[1, h] = grad.astype(BF16)
        send_result(1, h).start()

    def query_grads(h):
        take(send_dq, h)
        total = dq_own[h] + dq_in[h, 0].astype(F32) + dq_in[h, 1].astype(F32)
        grad, gain = norm_back((total * SCALE).T, q_raw[h].astype(F32), gains[0])
        gain_acc[0:1] += gain
        results[0, h] = grad.astype(BF16)
        send_result(0, h).start()

    gain_acc[...] = jnp.zeros_like(gain_acc)
    normalize(0)
    pl.semaphore_wait(barrier, len(greeted))
    give_pair(0)
    for h in range(1, AHEAD):
        normalize(h)
        give_pair(h)
    for h in range(AHEAD):
        normalize_key(h)

    def within(i):
        return (i >= 0) & (i < HEADS)

    def step(i, carry):
        @pl.when(within(i - TOTAL_LAG))
        def _():
            totals(i - TOTAL_LAG)

        @pl.when(within(i))
        def _():
            take(send_pair, i)
            scores(i)

        @pl.when(within(i + AHEAD))
        def _():
            normalize(i + AHEAD)
            give_pair(i + AHEAD)
            normalize_key(i + AHEAD)

        @pl.when(within(i - GRAD_LAG))
        def _():
            grads(i - GRAD_LAG)

        @pl.when(within(i - QUERY_LAG))
        def _():
            query_grads(i - QUERY_LAG)

        return carry

    lax.fori_loop(0, STEPS, step, 0)

    for axis, (mine, size, device) in enumerate(groups):
        gain_slots[axis, mine] = gain_acc[...]
        copies = [
            remote(
                gain_slots.at[axis, mine], gain_slots.at[axis, mine],
                gain_send.at[axis, j - 1], gain_recv.at[axis, j - 1], device(lax.rem(mine + j, size)),
            )
            for j in range(1, size)
        ]
        for copy in copies:
            copy.start()
        for j in range(1, size):
            sender = lax.rem(mine + size - j, size)
            remote(
                gain_slots.at[axis, mine], gain_slots.at[axis, sender],
                gain_send.at[axis, j - 1], gain_recv.at[axis, j - 1], device(lax.rem(mine + j, size)),
            ).wait_recv()
        for copy in copies:
            copy.wait_send()
        total = gain_slots[axis, 0]
        for j in range(1, size):
            total = total + gain_slots[axis, j]
        gain_acc[...] = total
    gain_out[...] = gain_acc[...] * (1.0 / math.sqrt(dps * seqs * TILE * HEADS))

    def finish(h, carry):
        for copy in (send_pair, send_stat, send_total, send_dq):
            for side in (0, 1):
                copy(h, side).wait_send()
        for part in range(3):
            send_result(part, h).wait()
        return carry

    lax.fori_loop(0, HEADS, finish, 0)


def solution(mesh):
    seqs, dps = mesh.shape["seq"], mesh.shape["dp"]
    zs = 4
    dma, vmem = pltpu.SemaphoreType.DMA, pltpu.VMEM

    def body(*refs):
        kernel(seqs, dps, zs, *refs)

    call = pl.pallas_call(
        body,
        out_shape=(
            jax.ShapeDtypeStruct((3, TILE, HEADS * DIM), BF16),
            jax.ShapeDtypeStruct((2, DIM), F32),
        ),
        in_specs=[pl.BlockSpec(memory_space=pl.ANY)] * 4
        + [pl.BlockSpec(memory_space=pltpu.VMEM), pl.BlockSpec(memory_space=pltpu.SMEM)],
        out_specs=(pl.BlockSpec(memory_space=pl.ANY), pl.BlockSpec(memory_space=pltpu.VMEM)),
        scratch_shapes=[
            vmem((HEADS, TILE, DIM), BF16),
            vmem((HEADS, TILE, DIM), BF16),
            vmem((HEADS, TILE, DIM), BF16),
            vmem((HEADS, 2, SPAN, DIM), BF16),
            vmem((HEADS, TILE, DIM), BF16),
            vmem((HEADS, DIM, TILE), BF16),
            vmem((SLOTS, TILE, SPAN), F32),
            vmem((SLOTS, TILE, SPAN), F32),
            vmem((2, TILE, SPAN), BF16),
            vmem((HEADS, 2, TILE), F32),
            vmem((HEADS, 2, 2, TILE), F32),
            vmem((HEADS, 2, 2, TILE), F32),
            vmem((HEADS, 2, TILE), F32),
            vmem((HEADS, 2, 2, TILE), F32),
            vmem((HEADS, 2, 2, TILE), F32),
            vmem((HEADS, DIM, TILE), F32),
            vmem((HEADS, 2, DIM, TILE), BF16),
            vmem((HEADS, 2, DIM, TILE), BF16),
            vmem((3, HEADS, TILE, DIM), BF16),
            vmem((2, DIM), F32),
            vmem((3, 4, 2, DIM), F32),
            dma((4, HEADS)),
        ]
        + [dma((HEADS, 2))] * 8
        + [dma((3, HEADS)), dma((3, HEADS)), dma((3, 3)), dma((3, 3))],
        compiler_params=pltpu.CompilerParams(
            collective_id=0, has_side_effects=True, vmem_limit_bytes=58 * 2**20
        ),
        cost_estimate=pl.CostEstimate(
            flops=10 * TILE * SPAN * HEADS * DIM,
            bytes_accessed=7 * 2 * TILE * HEADS * DIM,
            transcendentals=TILE * SPAN * HEADS,
        ),
    )

    def local(queries, keys, values, grad_out, norm_gains, kv_tiles):
        grads, gain_grads = call(
            queries[0, 0, 0], keys[0, 0, 0], values[0, 0, 0], grad_out[0, 0, 0],
            norm_gains[0], kv_tiles[0, 0],
        )
        return grads[None, :, None, None], gain_grads[None]

    tokens = P("pipe", "dp", "seq", None, None)
    return jax.shard_map(
        local,
        mesh=mesh,
        in_specs=(tokens,) * 4 + (P("pipe", None, None), P("pipe", "dp", "seq", None)),
        out_specs=(P("pipe", None, "dp", "seq", None, None), P("pipe", None, None)),
        check_vma=False,
    )
```

```python
import math

import jax
import jax.numpy as jnp
from jax import lax
from jax.experimental import pallas as pl
from jax.experimental.pallas import tpu as pltpu
from jax.sharding import PartitionSpec as P

HEADS = 12
DIM = 128
TILE = 384
SPAN = 3 * TILE
EPSILON = 1e-06
SCALE = DIM**-0.5
EXP2_SCALE = SCALE * math.log2(math.e)
MESH = pl.DeviceIdType.MESH
BF16, F32 = jnp.bfloat16, jnp.float32

SWAPPED = 2
KEPT = HEADS - SWAPPED
GRAD_LAG, AHEAD, DQ_FROM, Q_FROM, RATE = 2, 3, 9, 11, 2
SLOTS = GRAD_LAG + 1
STEPS = HEADS + GRAD_LAG


def over_rows(a, b):
    return lax.dot_general(a, b, (((1,), (1,)), ((), ())), preferred_element_type=F32)


def product(a, b):
    return lax.dot_general(a, b, (((1,), (0,)), ((), ())), preferred_element_type=F32)


def inverse_norm(x):
    return lax.rsqrt(jnp.mean(x * x, axis=-1, keepdims=True) + EPSILON)


def norm_back(grad_hat, x, gain, inverse):
    projected = jnp.sum(gain * grad_hat * x, axis=-1, keepdims=True)
    return inverse * (gain * grad_hat) - x * (inverse * inverse * inverse * projected * (1.0 / DIM))


def kernel(
    seqs, dps, zs,
    q_ref, k_ref, v_ref, g_ref, gain_ref, list_ref,
    out_ref, gain_out,
    q_raw, k_raw, v_in, pair, k_hat, k_turned, exps, gprobs, low,
    stat, stat_l, stat_r, stat_ll, stat_rr, masks, gains,
    dq_own, dq_out, dq_in, results, gain_acc, first_slots, gain_slots,
    load_sem, swap_send, swap_recv, in_send, in_recv, stat_send, stat_recv, info_send, info_recv, dq_send, dq_recv,
    out_send, out_recv, keep_sem, first_send, first_recv, gain_send, gain_recv,
):
    p, s, d = lax.axis_index("pipe"), lax.axis_index("seq"), lax.axis_index("dp")

    def at(q, step):
        return (q, lax.rem(s + seqs + step, seqs), d)

    left, right = at(p, -1), at(p, 1)
    sides = (left, right)
    across = at(1 - p, 0)
    xs = seqs // zs
    x, z = s // zs, lax.rem(s, zs)
    groups = (
        (x, xs, lambda i: (p, i * zs + z, d)),
        (z, zs, lambda i: (p, x * zs + i, d)),
    )

    def columns(h):
        return pl.ds(pl.multiple_of(h * DIM, DIM), DIM)

    def remote(source, target, send, recv, device):
        return pltpu.make_async_remote_copy(
            src_ref=source, dst_ref=target, send_sem=send, recv_sem=recv,
            device_id=device, device_id_type=MESH,
        )

    def places(h):
        return (
            (q_ref, q_raw.at[h]),
            (k_ref, k_raw.at[h]),
            (g_ref, pair.at[h, 1, pl.ds(TILE, TILE)]),
            (v_ref, v_in.at[h]),
        )

    def loads(h):
        return [
            pltpu.make_async_copy(source.at[:, columns(h)], target, load_sem.at[part, h])
            for part, (source, target) in enumerate(places(h))
        ]

    def swaps(h):
        return [
            remote(
                source.at[:, columns(h)], target,
                swap_send.at[part, h - KEPT], swap_recv.at[part, h - KEPT], across,
            )
            for part, (source, target) in enumerate(places(h))
        ]

    def start_loads(h, carry):
        for copy in loads(h):
            copy.start()
        return carry

    lax.fori_loop(0, KEPT, start_loads, 0)

    barrier = pltpu.get_barrier_semaphore()
    greeted = [at(p, -1), at(p, 1), at(p, -2), at(p, 2), at(1 - p, -1), at(1 - p, 0), at(1 - p, 1)]
    for j in range(1, dps):
        greeted += [(q, s, lax.rem(d + j, dps)) for q in (p, 1 - p)]
    for mine, size, device in groups:
        greeted += [device(lax.rem(mine + j, size)) for j in range(1, size)]
    for device in greeted:
        pl.semaphore_signal(barrier, inc=1, device_id=device, device_id_type=MESH)

    def names(tile):
        named = (list_ref[0, 0] == tile) | (list_ref[0, 1] == tile) | (list_ref[0, 2] == tile)
        return jnp.where(named, 1.0, 0.0).astype(F32)

    masks[0, 1, 0:1] = jnp.full((1, TILE), jnp.where(s > 0, names(s - 1), 0.0), F32)
    masks[0, 1, 1:2] = jnp.full((1, TILE), names(s + 1), F32)
    gains[0] = gain_ref[...]

    own_masks = masks.at[0, 1]
    infos = [
        remote(own_masks, masks.at[q, t], info_send.at[e], info_recv.at[e], device)
        for e, (q, t, device) in enumerate(
            (
                (0, 2, at(p, -1)), (0, 0, at(p, 1)),
                (1, 2, at(1 - p, -1)), (1, 0, at(1 - p, 1)), (1, 1, across),
            )
        )
    ]
    infos.append(remote(gains.at[0], gains.at[1], info_send.at[5], info_recv.at[5], across))

    def send_pair(h, side):
        return remote(
            pair.at[h, :, pl.ds(TILE, TILE)], pair.at[h, :, pl.ds(2 * TILE * (1 - side), TILE)],
            in_send.at[h, side], in_recv.at[h, 1 - side], sides[side],
        )

    def send_dq(h, side):
        return remote(
            dq_out.at[h, side], dq_in.at[h, 1 - side], dq_send.at[h, side], dq_recv.at[h, 1 - side], sides[side]
        )

    def send_stats(h):
        return [
            remote(source, target.at[h], stat_send.at[h, e], stat_recv.at[h, e], device)
            for e, (source, target, device) in enumerate(
                (
                    (stat.at[h, pl.ds(0, 2)], stat_r, left),
                    (stat.at[h, pl.ds(1, 2)], stat_l, right),
                    (stat.at[h, pl.ds(0, 1)], stat_rr, at(p, -2)),
                    (stat.at[h, pl.ds(2, 1)], stat_ll, at(p, 2)),
                )
            )
        ]

    def send_result(part, h):
        return remote(
            results.at[part, h], out_ref.at[part, :, columns(h)],
            out_send.at[part, h], out_recv.at[part, h], across,
        )

    def keep_result(part, h):
        return pltpu.make_async_copy(
            results.at[part, h], out_ref.at[part, :, columns(h)], keep_sem.at[part, h - KEPT]
        )

    def give_result(part, h):
        @pl.when(h < KEPT)
        def _():
            send_result(part, h).start()

        @pl.when(h >= KEPT)
        def _():
            keep_result(part, h).start()

    def segment(h):
        return jnp.where(h >= KEPT, 1, 0)

    def normalize(h):
        @pl.when(h < KEPT)
        def _():
            for copy in loads(h):
                copy.wait()

        @pl.when(h >= KEPT)
        def _():
            for copy in swaps(h):
                copy.wait_recv()

        q = q_raw[h].astype(F32)
        pair[h, 0, TILE : 2 * TILE] = (q * inverse_norm(q) * gains[segment(h), 0:1]).astype(BF16)

    def normalize_key(h):
        k = k_raw[h].astype(F32)
        hat = k * inverse_norm(k) * gains[segment(h), 1:2]
        k_hat[h] = hat.astype(BF16)
        k_turned[h] = hat.T.astype(BF16)

    def give_pair(h):
        for side in (0, 1):
            send_pair(h, side).start()

    def scores(h):
        for side in (0, 1):
            send_pair(h, side).wait_recv()
        slot = lax.rem(h, SLOTS)
        for b in range(3):
            span = slice(b * TILE, (b + 1) * TILE)
            e = jnp.exp2(over_rows(k_hat[h], pair[h, 0, span]) * EXP2_SCALE)
            g = over_rows(v_in[h], pair[h, 1, span])
            exps[slot, :, span] = e
            gprobs[slot, :, span] = g
            stat[h, b, 0:1] = jnp.sum(e, axis=0, keepdims=True)
            stat[h, b, 1:2] = jnp.sum(e * g, axis=0, keepdims=True)
        for copy in send_stats(h):
            copy.start()

    def grads(h):
        for copy in send_stats(h):
            copy.wait_recv()
        slot, seg = lax.rem(h, SLOTS), segment(h)
        to_left = [masks[seg, t, 0:1] for t in range(3)]
        to_right = [masks[seg, t, 1:2] for t in range(3)]
        sums = (
            stat[h, 0] * to_right[0] + stat_l[h, 0] + stat_ll[h, 0] * to_left[0],
            stat[h, 1] + stat_l[h, 1] * to_left[1] + stat_r[h, 0] * to_right[1],
            stat[h, 2] * to_left[2] + stat_r[h, 1] + stat_rr[h, 0] * to_right[2],
        )
        for b in range(3):
            span = slice(b * TILE, (b + 1) * TILE)
            inverse = 1.0 / sums[b][0:1]
            delta = sums[b][1:2] * inverse
            share = (inverse * to_right[0], inverse, inverse * to_left[2])[b]
            probs = exps[slot, :, span] * share
            low[0, :, span] = probs.astype(BF16)
            low[1, :, span] = (probs * (gprobs[slot, :, span] - delta)).astype(BF16)
        results[2, h] = product(low[0], pair[h, 1]).astype(BF16)
        give_result(2, h)
        grad_hat = product(low[1], pair[h, 0]) * SCALE
        k = k_raw[h].astype(F32)
        inverse = inverse_norm(k)
        results[1, h] = norm_back(grad_hat, k, gains[seg, 1:2], inverse).astype(BF16)
        give_result(1, h)
        turned = product(k_turned[h], low[1])
        dq_out[h, 0] = turned[:, :TILE].astype(BF16)
        dq_out[h, 1] = turned[:, 2 * TILE :].astype(BF16)
        dq_own[h] = turned[:, TILE : 2 * TILE]
        gain_acc[seg, 0:1] += jnp.sum(grad_hat * k_hat[h].astype(F32), axis=0, keepdims=True) / gains[seg, 0:1]
        gain_acc[seg, 1:2] += jnp.sum(grad_hat * (k * inverse), axis=0, keepdims=True)

    def give_dq(h, carry):
        for side in (0, 1):
            send_dq(h, side).start()
        return carry

    def query_grads(h, carry):
        for side in (0, 1):
            send_dq(h, side).wait_recv()
        total = dq_own[h] + dq_in[h, 0].astype(F32) + dq_in[h, 1].astype(F32)
        q = q_raw[h].astype(F32)
        grad = norm_back((total * SCALE).T, q, gains[segment(h), 0:1], inverse_norm(q))
        results[0, h] = grad.astype(BF16)
        give_result(0, h)
        return carry

    gain_acc[...] = jnp.zeros_like(gain_acc)
    normalize(0)
    pl.semaphore_wait(barrier, len(greeted))
    give_pair(0)
    for copy in infos:
        copy.start()
    for h in range(KEPT, HEADS):
        for copy in swaps(h):
            copy.start()
    for h in range(1, AHEAD):
        normalize(h)
        give_pair(h)
    for h in range(AHEAD):
        normalize_key(h)
    for copy in infos:
        copy.wait_recv()

    def given(i):
        return jnp.clip(jnp.minimum((i - DQ_FROM + 1) * RATE, i - GRAD_LAG + 1), 0, HEADS)

    def taken(i):
        return jnp.clip(jnp.minimum((i - Q_FROM + 1) * RATE, given(i - 1)), 0, HEADS)

    def step(i, carry):
        @pl.when(i < HEADS)
        def _():
            scores(i)

        @pl.when(i + AHEAD < HEADS)
        def _():
            normalize(i + AHEAD)
            give_pair(i + AHEAD)
            normalize_key(i + AHEAD)

        @pl.when(i >= GRAD_LAG)
        def _():
            grads(i - GRAD_LAG)

        lax.fori_loop(given(i - 1), given(i), give_dq, 0)
        lax.fori_loop(taken(i - 1), taken(i), query_grads, 0)
        return carry

    lax.fori_loop(0, STEPS, step, 0)
    lax.fori_loop(given(STEPS - 1), HEADS, give_dq, 0)

    def first(j, other):
        to, sender = lax.rem(d + j, dps), lax.rem(d + dps - j, dps)
        copy = remote(
            gain_acc.at[other], first_slots.at[other, d], first_send.at[other, j], first_recv.at[other, j],
            (1 - p if other else p, s, to),
        )
        arrival = remote(
            gain_acc.at[other], first_slots.at[other, sender], first_send.at[other, j], first_recv.at[other, j],
            (1 - p if other else p, s, to),
        )
        return copy, arrival

    def later(axis, j):
        mine, size, device = groups[axis]
        to, sender = device(lax.rem(mine + j, size)), lax.rem(mine + size - j, size)
        return [
            remote(
                gain_slots.at[axis, mine], gain_slots.at[axis, slot],
                gain_send.at[axis, j - 1], gain_recv.at[axis, j - 1], to,
            )
            for slot in (mine, sender)
        ]

    rounds = [[first(j, other) for other in (0, 1) for j in range(1 - other, dps)]]
    rounds += [[later(axis, j) for j in range(1, groups[axis][1])] for axis in (0, 1)]

    def begin(r, value):
        if r == 0:
            first_slots[0, d] = value
        else:
            gain_slots[r - 1, groups[r - 1][0]] = value
        for copy, _ in rounds[r]:
            copy.start()

    def end(r):
        for _, arrival in rounds[r]:
            arrival.wait_recv()
        for copy, _ in rounds[r]:
            copy.wait_send()
        if r == 0:
            slots = [first_slots[other, j] for other in (0, 1) for j in range(dps)]
        else:
            slots = [gain_slots[r - 1, j] for j in range(groups[r - 1][1])]
        total = slots[0]
        for slot in slots[1:]:
            total = total + slot
        return total

    begin(0, gain_acc[0])
    done, rest = taken(STEPS - 1), HEADS - taken(STEPS - 1)
    marks = [done, done + rest // 2, done + rest * 3 // 4, HEADS]
    for r in range(3):
        lax.fori_loop(marks[r], marks[r + 1], query_grads, 0)
        total = end(r)
        if r < 2:
            begin(r + 1, total)
        else:
            gain_out[...] = total * (1.0 / math.sqrt(dps * seqs * TILE * HEADS))

    for copy in infos:
        copy.wait_send()

    def finish(h, carry):
        for side in (0, 1):
            send_pair(h, side).wait_send()
            send_dq(h, side).wait_send()
        for copy in send_stats(h):
            copy.wait_send()

        @pl.when(h < KEPT)
        def _():
            for part in range(3):
                send_result(part, h).wait()

        @pl.when(h >= KEPT)
        def _():
            for copy in swaps(h):
                copy.wait_send()
            for part in range(3):
                keep_result(part, h).wait()

        return carry

    lax.fori_loop(0, HEADS, finish, 0)


def solution(mesh):
    seqs, dps = mesh.shape["seq"], mesh.shape["dp"]
    zs = 4
    dma, vmem = pltpu.SemaphoreType.DMA, pltpu.VMEM

    def body(*refs):
        kernel(seqs, dps, zs, *refs)

    call = pl.pallas_call(
        body,
        out_shape=(
            pltpu.VMEM((3, TILE, HEADS * DIM), BF16),
            jax.ShapeDtypeStruct((2, DIM), F32),
        ),
        in_specs=[pl.BlockSpec(memory_space=pl.ANY)] * 4
        + [pl.BlockSpec(memory_space=pltpu.VMEM), pl.BlockSpec(memory_space=pltpu.SMEM)],
        out_specs=(pl.BlockSpec(memory_space=pltpu.VMEM), pl.BlockSpec(memory_space=pltpu.VMEM)),
        scratch_shapes=[
            vmem((HEADS, TILE, DIM), BF16),
            vmem((HEADS, TILE, DIM), BF16),
            vmem((HEADS, TILE, DIM), BF16),
            vmem((HEADS, 2, SPAN, DIM), BF16),
            vmem((HEADS, TILE, DIM), BF16),
            vmem((HEADS, DIM, TILE), BF16),
            vmem((SLOTS, TILE, SPAN), F32),
            vmem((SLOTS, TILE, SPAN), F32),
            vmem((2, TILE, SPAN), BF16),
            vmem((HEADS, 3, 2, TILE), F32),
            vmem((HEADS, 2, 2, TILE), F32),
            vmem((HEADS, 2, 2, TILE), F32),
            vmem((HEADS, 1, 2, TILE), F32),
            vmem((HEADS, 1, 2, TILE), F32),
            vmem((2, 3, 2, TILE), F32),
            vmem((2, 2, DIM), F32),
            vmem((HEADS, DIM, TILE), F32),
            vmem((HEADS, 2, DIM, TILE), BF16),
            vmem((HEADS, 2, DIM, TILE), BF16),
            vmem((3, HEADS, TILE, DIM), BF16),
            vmem((2, 2, DIM), F32),
            vmem((2, dps, 2, DIM), F32),
            vmem((2, 4, 2, DIM), F32),
            dma((4, HEADS)),
            dma((4, SWAPPED)),
            dma((4, SWAPPED)),
            dma((HEADS, 2)),
            dma((HEADS, 2)),
            dma((HEADS, 4)),
            dma((HEADS, 4)),
            dma((6,)),
            dma((6,)),
            dma((HEADS, 2)),
            dma((HEADS, 2)),
            dma((3, HEADS)),
            dma((3, HEADS)),
            dma((3, SWAPPED)),
            dma((2, dps)),
            dma((2, dps)),
            dma((2, 3)),
            dma((2, 3)),
        ],
        compiler_params=pltpu.CompilerParams(
            collective_id=0, has_side_effects=True, vmem_limit_bytes=58 * 2**20
        ),
        cost_estimate=pl.CostEstimate(
            flops=10 * TILE * SPAN * HEADS * DIM,
            bytes_accessed=7 * 2 * TILE * HEADS * DIM,
            transcendentals=TILE * SPAN * HEADS,
        ),
    )

    def local(queries, keys, values, grad_out, norm_gains, kv_tiles):
        grads, gain_grads = call(
            queries[0, 0, 0], keys[0, 0, 0], values[0, 0, 0], grad_out[0, 0, 0],
            norm_gains[0], kv_tiles[0, 0],
        )
        return grads[None, :, None, None], gain_grads[None]

    tokens = P("pipe", "dp", "seq", None, None)
    return jax.shard_map(
        local,
        mesh=mesh,
        in_specs=(tokens,) * 4 + (P("pipe", None, None), P("pipe", "dp", "seq", None)),
        out_specs=(P("pipe", None, "dp", "seq", None, None), P("pipe", None, None)),
        check_vma=False,
    )
```

```python
import math

import jax
import jax.numpy as jnp
from jax import lax
from jax.experimental import pallas as pl
from jax.experimental.pallas import tpu as pltpu
from jax.sharding import PartitionSpec as P

HEADS = 12
DIM = 128
TILE = 384
SPAN = 3 * TILE
EPSILON = 1e-06
SCALE = DIM**-0.5
EXP2_SCALE = SCALE * math.log2(math.e)
MESH = pl.DeviceIdType.MESH
BF16, F32 = jnp.bfloat16, jnp.float32

SWAPPED = 3
KEPT = HEADS - SWAPPED
GRAD_LAG, AHEAD, DQ_FROM, RATE, EARLY, WAIT = 2, 3, 9, 2, 0, 3
SLOTS = GRAD_LAG + 1
STEPS = HEADS + GRAD_LAG


def over_rows(a, b):
    return lax.dot_general(a, b, (((1,), (1,)), ((), ())), preferred_element_type=F32)


def product(a, b):
    return lax.dot_general(a, b, (((1,), (0,)), ((), ())), preferred_element_type=F32)


def inverse_norm(x):
    return lax.rsqrt(jnp.mean(x * x, axis=-1, keepdims=True) + EPSILON)


def norm_back(grad_hat, x, gain, inverse):
    projected = jnp.sum(gain * grad_hat * x, axis=-1, keepdims=True)
    return inverse * (gain * grad_hat) - x * (inverse * inverse * inverse * projected * (1.0 / DIM))


def kernel(
    seqs, dps, zs,
    q_ref, k_ref, v_ref, g_ref, gain_ref, list_ref,
    out_ref, gain_out,
    q_raw, k_raw, v_in, pair, k_hat, k_turned, exps, gprobs, low,
    stat, stat_l, stat_r, stat_ll, stat_rr, masks, gains,
    dq_own, dq_out, dq_in, results, gain_acc, first_slots, gain_slots,
    load_sem, swap_send, swap_recv, in_send, in_recv, stat_send, stat_recv, info_send, info_recv, dq_send, dq_recv,
    out_send, out_recv, first_send, first_recv, gain_send, gain_recv,
):
    p, s, d = lax.axis_index("pipe"), lax.axis_index("seq"), lax.axis_index("dp")

    def at(q, step):
        return (q, lax.rem(s + seqs + step, seqs), d)

    left, right = at(p, -1), at(p, 1)
    sides = (left, right)
    across = at(1 - p, 0)
    xs = seqs // zs
    x, z = s // zs, lax.rem(s, zs)
    groups = (
        (x, xs, lambda i: (p, i * zs + z, d)),
        (z, zs, lambda i: (p, x * zs + i, d)),
    )

    def columns(h):
        return pl.ds(pl.multiple_of(h * DIM, DIM), DIM)

    def remote(source, target, send, recv, device):
        return pltpu.make_async_remote_copy(
            src_ref=source, dst_ref=target, send_sem=send, recv_sem=recv,
            device_id=device, device_id_type=MESH,
        )

    def places(h):
        return (
            (q_ref, q_raw.at[h]),
            (k_ref, k_raw.at[h]),
            (g_ref, pair.at[h, 1, pl.ds(TILE, TILE)]),
            (v_ref, v_in.at[h]),
        )

    def loads(h):
        return [
            pltpu.make_async_copy(source.at[:, columns(h)], target, load_sem.at[part, h])
            for part, (source, target) in enumerate(places(h))
        ]

    def swaps(h):
        return [
            remote(
                source.at[:, columns(h)], target,
                swap_send.at[part], swap_recv.at[part, h - KEPT], across,
            )
            for part, (source, target) in enumerate(places(h))
        ]

    def start_loads(h, carry):
        for copy in loads(h):
            copy.start()
        return carry

    lax.fori_loop(0, KEPT, start_loads, 0)

    barrier = pltpu.get_barrier_semaphore()
    greeted = [at(p, -1), at(p, 1), at(p, -2), at(p, 2), at(1 - p, -1), at(1 - p, 0), at(1 - p, 1)]
    for j in range(1, dps):
        greeted += [(q, s, lax.rem(d + j, dps)) for q in (p, 1 - p)]
    for mine, size, device in groups:
        greeted += [device(lax.rem(mine + j, size)) for j in range(1, size)]
    for device in greeted:
        pl.semaphore_signal(barrier, inc=1, device_id=device, device_id_type=MESH)

    def names(tile):
        named = (list_ref[0, 0] == tile) | (list_ref[0, 1] == tile) | (list_ref[0, 2] == tile)
        return jnp.where(named, 1.0, 0.0).astype(F32)

    masks[0, 1, 0:1] = jnp.full((1, TILE), jnp.where(s > 0, names(s - 1), 0.0), F32)
    masks[0, 1, 1:2] = jnp.full((1, TILE), names(s + 1), F32)
    gains[0] = gain_ref[...]

    own_masks = masks.at[0, 1]
    infos = [
        remote(own_masks, masks.at[q, t], info_send.at[e], info_recv.at[e], device)
        for e, (q, t, device) in enumerate(
            (
                (0, 2, at(p, -1)), (0, 0, at(p, 1)),
                (1, 2, at(1 - p, -1)), (1, 0, at(1 - p, 1)), (1, 1, across),
            )
        )
    ]
    infos.append(remote(gains.at[0], gains.at[1], info_send.at[5], info_recv.at[5], across))

    def send_pair(h, side):
        return remote(
            pair.at[h, :, pl.ds(TILE, TILE)], pair.at[h, :, pl.ds(2 * TILE * (1 - side), TILE)],
            in_send.at[side], in_recv.at[h, 1 - side], sides[side],
        )

    def send_dq(h, side):
        return remote(
            dq_out.at[h, side], dq_in.at[h, 1 - side], dq_send.at[side], dq_recv.at[h, 1 - side], sides[side]
        )

    def send_stats(h):
        return [
            remote(source, target.at[h], stat_send.at[e], stat_recv.at[h, e], device)
            for e, (source, target, device) in enumerate(
                (
                    (stat.at[h, pl.ds(0, 2)], stat_r, left),
                    (stat.at[h, pl.ds(1, 2)], stat_l, right),
                    (stat.at[h, pl.ds(0, 1)], stat_rr, at(p, -2)),
                    (stat.at[h, pl.ds(2, 1)], stat_ll, at(p, 2)),
                )
            )
        ]

    def send_result(part, h):
        return remote(
            results.at[part, h], out_ref.at[part, :, columns(h)],
            out_send.at[0], out_recv.at[0], across,
        )

    def give_result(part, h, value):
        @pl.when(h < KEPT)
        def _():
            results[part, h] = value
            send_result(part, h).start()

        @pl.when(h >= KEPT)
        def _():
            out_ref[part, :, columns(h)] = value

    def segment(h):
        return jnp.where(h >= KEPT, 1, 0)

    def normalize(h):
        @pl.when(h < KEPT)
        def _():
            for copy in loads(h):
                copy.wait()

        @pl.when(h >= KEPT)
        def _():
            for copy in swaps(h):
                copy.wait_recv()

        q = q_raw[h].astype(F32)
        pair[h, 0, TILE : 2 * TILE] = (q * inverse_norm(q) * gains[segment(h), 0:1]).astype(BF16)

    def normalize_key(h):
        k = k_raw[h].astype(F32)
        hat = k * inverse_norm(k) * gains[segment(h), 1:2]
        k_hat[h] = hat.astype(BF16)
        k_turned[h] = hat.T.astype(BF16)

    def give_pair(h):
        for side in (0, 1):
            send_pair(h, side).start()

    def scores(h):
        for side in (0, 1):
            send_pair(h, side).wait_recv()
        slot = lax.rem(h, SLOTS)
        for b in range(3):
            span = slice(b * TILE, (b + 1) * TILE)
            e = jnp.exp2(over_rows(k_hat[h], pair[h, 0, span]) * EXP2_SCALE)
            g = over_rows(v_in[h], pair[h, 1, span])
            exps[slot, :, span] = e
            gprobs[slot, :, span] = g
            stat[h, b, 0:1] = jnp.sum(e, axis=0, keepdims=True)
            stat[h, b, 1:2] = jnp.sum(e * g, axis=0, keepdims=True)
        for copy in send_stats(h):
            copy.start()

    def grads(h):
        for copy in send_stats(h):
            copy.wait_recv()
        slot, seg = lax.rem(h, SLOTS), segment(h)
        to_left = [masks[seg, t, 0:1] for t in range(3)]
        to_right = [masks[seg, t, 1:2] for t in range(3)]
        sums = (
            stat[h, 0] * to_right[0] + stat_l[h, 0] + stat_ll[h, 0] * to_left[0],
            stat[h, 1] + stat_l[h, 1] * to_left[1] + stat_r[h, 0] * to_right[1],
            stat[h, 2] * to_left[2] + stat_r[h, 1] + stat_rr[h, 0] * to_right[2],
        )
        for b in range(3):
            span = slice(b * TILE, (b + 1) * TILE)
            inverse = 1.0 / sums[b][0:1]
            delta = sums[b][1:2] * inverse
            share = (inverse * to_right[0], inverse, inverse * to_left[2])[b]
            probs = exps[slot, :, span] * share
            low[0, :, span] = probs.astype(BF16)
            low[1, :, span] = (probs * (gprobs[slot, :, span] - delta)).astype(BF16)
        give_result(2, h, product(low[0], pair[h, 1]).astype(BF16))
        grad_hat = product(low[1], pair[h, 0]) * SCALE
        k = k_raw[h].astype(F32)
        inverse = inverse_norm(k)
        give_result(1, h, norm_back(grad_hat, k, gains[seg, 1:2], inverse).astype(BF16))
        turned = product(k_turned[h], low[1])
        dq_out[h, 0] = turned[:, :TILE].astype(BF16)
        dq_out[h, 1] = turned[:, 2 * TILE :].astype(BF16)
        dq_own[h] = turned[:, TILE : 2 * TILE]
        gain_acc[seg, 0:1] += jnp.sum(grad_hat * k_hat[h].astype(F32), axis=0, keepdims=True) / gains[seg, 0:1]
        gain_acc[seg, 1:2] += jnp.sum(grad_hat * (k * inverse), axis=0, keepdims=True)

    def give_dq(h, carry):
        for side in (0, 1):
            send_dq(h, side).start()
        return carry

    def query_grads(h, carry):
        for side in (0, 1):
            send_dq(h, side).wait_recv()
        total = dq_own[h] + dq_in[h, 0].astype(F32) + dq_in[h, 1].astype(F32)
        q = q_raw[h].astype(F32)
        grad = norm_back((total * SCALE).T, q, gains[segment(h), 0:1], inverse_norm(q))
        give_result(0, h, grad.astype(BF16))
        return carry

    gain_acc[...] = jnp.zeros_like(gain_acc)
    normalize(0)
    pl.semaphore_wait(barrier, len(greeted))
    give_pair(0)
    for copy in infos:
        copy.start()
    for h in range(KEPT, HEADS):
        for copy in swaps(h):
            copy.start()
    for h in range(1, AHEAD):
        normalize(h)
        give_pair(h)
    for h in range(AHEAD):
        normalize_key(h)

    def given(i):
        early = (jnp.clip(i - GRAD_LAG, 0, HEADS) * EARLY) // 6
        late = (i - DQ_FROM + 1) * RATE
        return jnp.clip(jnp.minimum(jnp.maximum(early, late), i - GRAD_LAG + 1), 0, HEADS)

    def taken(i):
        return given(i - WAIT)

    def step(i, carry):
        @pl.when(i < HEADS)
        def _():
            scores(i)

        @pl.when(i + AHEAD < HEADS)
        def _():
            normalize(i + AHEAD)
            give_pair(i + AHEAD)
            normalize_key(i + AHEAD)

        @pl.when(i == 0)
        def _():
            for copy in infos:
                copy.wait_recv()

        @pl.when(i >= GRAD_LAG)
        def _():
            grads(i - GRAD_LAG)

        lax.fori_loop(given(i - 1), given(i), give_dq, 0)
        lax.fori_loop(taken(i - 1), taken(i), query_grads, 0)
        return carry

    lax.fori_loop(0, STEPS, step, 0)
    lax.fori_loop(given(STEPS - 1), HEADS, give_dq, 0)

    def first(j, other):
        to, sender = lax.rem(d + j, dps), lax.rem(d + dps - j, dps)
        copy = remote(
            gain_acc.at[other], first_slots.at[other, d], first_send.at[other, j], first_recv.at[other, j],
            (1 - p if other else p, s, to),
        )
        arrival = remote(
            gain_acc.at[other], first_slots.at[other, sender], first_send.at[other, j], first_recv.at[other, j],
            (1 - p if other else p, s, to),
        )
        return copy, arrival

    def later(axis, j):
        mine, size, device = groups[axis]
        to, sender = device(lax.rem(mine + j, size)), lax.rem(mine + size - j, size)
        return [
            remote(
                gain_slots.at[axis, mine], gain_slots.at[axis, slot],
                gain_send.at[axis, j - 1], gain_recv.at[axis, j - 1], to,
            )
            for slot in (mine, sender)
        ]

    rounds = [[first(j, other) for other in (0, 1) for j in range(1 - other, dps)]]
    rounds += [[later(axis, j) for j in range(1, groups[axis][1])] for axis in (0, 1)]

    def begin(r, value):
        if r == 0:
            first_slots[0, d] = value
        else:
            gain_slots[r - 1, groups[r - 1][0]] = value
        for copy, _ in rounds[r]:
            copy.start()

    def end(r):
        for _, arrival in rounds[r]:
            arrival.wait_recv()
        for copy, _ in rounds[r]:
            copy.wait_send()
        if r == 0:
            slots = [first_slots[other, j] for other in (0, 1) for j in range(dps)]
        else:
            slots = [gain_slots[r - 1, j] for j in range(groups[r - 1][1])]
        total = slots[0]
        for slot in slots[1:]:
            total = total + slot
        return total

    begin(0, gain_acc[0])
    done, rest = taken(STEPS - 1), HEADS - taken(STEPS - 1)
    marks = [done, done + rest // 2, done + rest * 3 // 4, HEADS]
    for r in range(3):
        lax.fori_loop(marks[r], marks[r + 1], query_grads, 0)
        total = end(r)
        if r < 2:
            begin(r + 1, total)
        else:
            gain_out[...] = total * (1.0 / math.sqrt(dps * seqs * TILE * HEADS))

    for copy in infos:
        copy.wait_send()

    kept, swapped = pl.ds(0, KEPT * DIM), pl.ds(KEPT * DIM, SWAPPED * DIM)
    for side in (0, 1):
        own = pair.at[:, :, pl.ds(TILE, TILE)]
        remote(own, own, in_send.at[side], in_send.at[side], sides[side]).wait_send()
        own = dq_out.at[:, side]
        remote(own, own, dq_send.at[side], dq_send.at[side], sides[side]).wait_send()
    for e, own in enumerate(
        (stat.at[:, pl.ds(0, 2)], stat.at[:, pl.ds(1, 2)], stat.at[:, pl.ds(0, 1)], stat.at[:, pl.ds(2, 1)])
    ):
        remote(own, own, stat_send.at[e], stat_send.at[e], left).wait_send()
    for part, source in enumerate((q_ref, k_ref, g_ref, v_ref)):
        own = source.at[:, swapped]
        remote(own, own, swap_send.at[part], swap_send.at[part], across).wait_send()
    final = remote(results, out_ref.at[:, :, kept], out_send.at[0], out_recv.at[0], across)
    final.wait_send()
    final.wait_recv()


def solution(mesh):
    seqs, dps = mesh.shape["seq"], mesh.shape["dp"]
    zs = 4
    dma, vmem = pltpu.SemaphoreType.DMA, pltpu.VMEM

    def body(*refs):
        kernel(seqs, dps, zs, *refs)

    call = pl.pallas_call(
        body,
        out_shape=(
            pltpu.VMEM((3, TILE, HEADS * DIM), BF16),
            jax.ShapeDtypeStruct((2, DIM), F32),
        ),
        in_specs=[pl.BlockSpec(memory_space=pl.ANY)] * 4
        + [pl.BlockSpec(memory_space=pltpu.VMEM), pl.BlockSpec(memory_space=pltpu.SMEM)],
        out_specs=(pl.BlockSpec(memory_space=pltpu.VMEM), pl.BlockSpec(memory_space=pltpu.VMEM)),
        scratch_shapes=[
            vmem((HEADS, TILE, DIM), BF16),
            vmem((HEADS, TILE, DIM), BF16),
            vmem((HEADS, TILE, DIM), BF16),
            vmem((HEADS, 2, SPAN, DIM), BF16),
            vmem((HEADS, TILE, DIM), BF16),
            vmem((HEADS, DIM, TILE), BF16),
            vmem((SLOTS, TILE, SPAN), F32),
            vmem((SLOTS, TILE, SPAN), F32),
            vmem((2, TILE, SPAN), BF16),
            vmem((HEADS, 3, 2, TILE), F32),
            vmem((HEADS, 2, 2, TILE), F32),
            vmem((HEADS, 2, 2, TILE), F32),
            vmem((HEADS, 1, 2, TILE), F32),
            vmem((HEADS, 1, 2, TILE), F32),
            vmem((2, 3, 2, TILE), F32),
            vmem((2, 2, DIM), F32),
            vmem((HEADS, DIM, TILE), F32),
            vmem((HEADS, 2, DIM, TILE), BF16),
            vmem((HEADS, 2, DIM, TILE), BF16),
            vmem((3, KEPT, TILE, DIM), BF16),
            vmem((2, 2, DIM), F32),
            vmem((2, dps, 2, DIM), F32),
            vmem((2, 4, 2, DIM), F32),
            dma((4, HEADS)),
            dma((4,)),
            dma((4, SWAPPED)),
            dma((2,)),
            dma((HEADS, 2)),
            dma((4,)),
            dma((HEADS, 4)),
            dma((6,)),
            dma((6,)),
            dma((2,)),
            dma((HEADS, 2)),
            dma((1,)),
            dma((1,)),
            dma((2, dps)),
            dma((2, dps)),
            dma((2, 3)),
            dma((2, 3)),
        ],
        compiler_params=pltpu.CompilerParams(
            collective_id=0, has_side_effects=True, vmem_limit_bytes=58 * 2**20
        ),
        cost_estimate=pl.CostEstimate(
            flops=10 * TILE * SPAN * HEADS * DIM,
            bytes_accessed=7 * 2 * TILE * HEADS * DIM,
            transcendentals=TILE * SPAN * HEADS,
        ),
    )

    def local(queries, keys, values, grad_out, norm_gains, kv_tiles):
        grads, gain_grads = call(
            queries[0, 0, 0], keys[0, 0, 0], values[0, 0, 0], grad_out[0, 0, 0],
            norm_gains[0], kv_tiles[0, 0],
        )
        return grads[None, :, None, None], gain_grads[None]

    tokens = P("pipe", "dp", "seq", None, None)
    return jax.shard_map(
        local,
        mesh=mesh,
        in_specs=(tokens,) * 4 + (P("pipe", None, None), P("pipe", "dp", "seq", None)),
        out_specs=(P("pipe", None, "dp", "seq", None, None), P("pipe", None, None)),
        check_vma=False,
    )
```

```python
import math

import jax
import jax.numpy as jnp
from jax import lax
from jax.experimental import pallas as pl
from jax.experimental.pallas import tpu as pltpu
from jax.sharding import PartitionSpec as P

HEADS = 12
DIM = 128
TILE = 384
SPAN = 3 * TILE
EPSILON = 1e-06
SCALE = DIM**-0.5
EXP2_SCALE = SCALE * math.log2(math.e)
MESH = pl.DeviceIdType.MESH
BF16, F32 = jnp.bfloat16, jnp.float32

SWAPPED = 3
KEPT = HEADS - SWAPPED
GRAD_LAG, AHEAD, DQ_FROM, RATE, EARLY, WAIT = 2, 3, 9, 2, 0, 3
SLOTS = GRAD_LAG + 1
STEPS = HEADS + GRAD_LAG


def over_rows(a, b):
    return lax.dot_general(a, b, (((1,), (1,)), ((), ())), preferred_element_type=F32)


def product(a, b):
    return lax.dot_general(a, b, (((1,), (0,)), ((), ())), preferred_element_type=F32)


def inverse_norm(x):
    return lax.rsqrt(jnp.mean(x * x, axis=-1, keepdims=True) + EPSILON)


def norm_back(grad_hat, x, gain, inverse):
    projected = jnp.sum(gain * grad_hat * x, axis=-1, keepdims=True)
    return inverse * (gain * grad_hat) - x * (inverse * inverse * inverse * projected * (1.0 / DIM))


def kernel(
    seqs, dps, zs,
    q_ref, k_ref, v_ref, g_ref, gain_ref, list_ref,
    out_ref, gain_out,
    q_raw, k_raw, v_in, pair, k_hat, k_turned, exps, gprobs, low,
    stat, stat_l, stat_r, stat_ll, stat_rr, masks, gains,
    dq_own, dq_out, dq_in, results, gain_acc, first_slots, gain_slots,
    load_sem, swap_send, swap_recv, in_send, in_recv, stat_send, stat_recv, info_send, info_recv, dq_send, dq_recv,
    out_send, out_recv, first_send, first_recv, gain_send, gain_recv,
):
    p, s, d = lax.axis_index("pipe"), lax.axis_index("seq"), lax.axis_index("dp")

    def at(q, step):
        return (q, lax.rem(s + seqs + step, seqs), d)

    left, right = at(p, -1), at(p, 1)
    sides = (left, right)
    across = at(1 - p, 0)
    xs = seqs // zs
    x, z = s // zs, lax.rem(s, zs)
    groups = (
        (x, xs, lambda i: (p, i * zs + z, d)),
        (z, zs, lambda i: (p, x * zs + i, d)),
    )

    def columns(h):
        return pl.ds(pl.multiple_of(h * DIM, DIM), DIM)

    def remote(source, target, send, recv, device):
        return pltpu.make_async_remote_copy(
            src_ref=source, dst_ref=target, send_sem=send, recv_sem=recv,
            device_id=device, device_id_type=MESH,
        )

    def places(h):
        return (
            (q_ref, q_raw.at[h]),
            (k_ref, k_raw.at[h]),
            (g_ref, pair.at[h, 1, pl.ds(TILE, TILE)]),
            (v_ref, v_in.at[h]),
        )

    def loads(h):
        return [
            pltpu.make_async_copy(source.at[:, columns(h)], target, load_sem.at[part, h])
            for part, (source, target) in enumerate(places(h))
        ]

    def swaps(h):
        return [
            remote(
                source.at[:, columns(h)], target,
                swap_send.at[part], swap_recv.at[part, h - KEPT], across,
            )
            for part, (source, target) in enumerate(places(h))
        ]

    def start_loads(h, carry):
        for copy in loads(h):
            copy.start()
        return carry

    barrier = pltpu.get_barrier_semaphore()
    greeted = [at(p, -1), at(p, 1), at(p, -2), at(p, 2), at(1 - p, -1), at(1 - p, 0), at(1 - p, 1)]
    for j in range(1, dps):
        greeted += [(q, s, lax.rem(d + j, dps)) for q in (p, 1 - p)]
    for mine, size, device in groups:
        greeted += [device(lax.rem(mine + j, size)) for j in range(1, size)]
    for device in greeted:
        pl.semaphore_signal(barrier, inc=1, device_id=device, device_id_type=MESH)
    start_loads(0, 0)

    def names(tile):
        named = (list_ref[0, 0] == tile) | (list_ref[0, 1] == tile) | (list_ref[0, 2] == tile)
        return jnp.where(named, 1.0, 0.0).astype(F32)

    masks[0, 1, 0:1] = jnp.full((1, TILE), jnp.where(s > 0, names(s - 1), 0.0), F32)
    masks[0, 1, 1:2] = jnp.full((1, TILE), names(s + 1), F32)
    gains[0] = gain_ref[...]

    own_masks = masks.at[0, 1]
    infos = [
        remote(own_masks, masks.at[q, t], info_send.at[e], info_recv.at[e], device)
        for e, (q, t, device) in enumerate(
            (
                (0, 2, at(p, -1)), (0, 0, at(p, 1)),
                (1, 2, at(1 - p, -1)), (1, 0, at(1 - p, 1)), (1, 1, across),
            )
        )
    ]
    infos.append(remote(gains.at[0], gains.at[1], info_send.at[5], info_recv.at[5], across))

    def send_pair(h, side):
        return remote(
            pair.at[h, :, pl.ds(TILE, TILE)], pair.at[h, :, pl.ds(2 * TILE * (1 - side), TILE)],
            in_send.at[side], in_recv.at[h, 1 - side], sides[side],
        )

    def send_dq(h, side):
        return remote(
            dq_out.at[h, side], dq_in.at[h, 1 - side], dq_send.at[side], dq_recv.at[h, 1 - side], sides[side]
        )

    def send_stats(h):
        return [
            remote(source, target.at[h], stat_send.at[e], stat_recv.at[h, e], device)
            for e, (source, target, device) in enumerate(
                (
                    (stat.at[h, pl.ds(0, 2)], stat_r, left),
                    (stat.at[h, pl.ds(1, 2)], stat_l, right),
                    (stat.at[h, pl.ds(0, 1)], stat_rr, at(p, -2)),
                    (stat.at[h, pl.ds(2, 1)], stat_ll, at(p, 2)),
                )
            )
        ]

    def send_result(part, h):
        return remote(
            results.at[part, h], out_ref.at[part, :, columns(h)],
            out_send.at[0], out_recv.at[0], across,
        )

    def give_result(part, h, value):
        @pl.when(h < KEPT)
        def _():
            results[part, h] = value
            send_result(part, h).start()

        @pl.when(h >= KEPT)
        def _():
            out_ref[part, :, columns(h)] = value

    def segment(h):
        return jnp.where(h >= KEPT, 1, 0)

    def normalize(h):
        @pl.when(h < KEPT)
        def _():
            for copy in loads(h):
                copy.wait()

        @pl.when(h >= KEPT)
        def _():
            for copy in swaps(h):
                copy.wait_recv()

        q = q_raw[h].astype(F32)
        pair[h, 0, TILE : 2 * TILE] = (q * inverse_norm(q) * gains[segment(h), 0:1]).astype(BF16)

    def normalize_key(h):
        k = k_raw[h].astype(F32)
        hat = k * inverse_norm(k) * gains[segment(h), 1:2]
        k_hat[h] = hat.astype(BF16)
        k_turned[h] = hat.T.astype(BF16)

    def give_pair(h):
        for side in (0, 1):
            send_pair(h, side).start()

    def scores(h):
        for side in (0, 1):
            send_pair(h, side).wait_recv()
        slot = lax.rem(h, SLOTS)
        for b in range(3):
            span = slice(b * TILE, (b + 1) * TILE)
            e = jnp.exp2(over_rows(k_hat[h], pair[h, 0, span]) * EXP2_SCALE)
            g = over_rows(v_in[h], pair[h, 1, span])
            exps[slot, :, span] = e
            gprobs[slot, :, span] = g
            stat[h, b, 0:1] = jnp.sum(e, axis=0, keepdims=True)
            stat[h, b, 1:2] = jnp.sum(e * g, axis=0, keepdims=True)
        for copy in send_stats(h):
            copy.start()

    def grads(h):
        for copy in send_stats(h):
            copy.wait_recv()
        slot, seg = lax.rem(h, SLOTS), segment(h)
        to_left = [masks[seg, t, 0:1] for t in range(3)]
        to_right = [masks[seg, t, 1:2] for t in range(3)]
        sums = (
            stat[h, 0] * to_right[0] + stat_l[h, 0] + stat_ll[h, 0] * to_left[0],
            stat[h, 1] + stat_l[h, 1] * to_left[1] + stat_r[h, 0] * to_right[1],
            stat[h, 2] * to_left[2] + stat_r[h, 1] + stat_rr[h, 0] * to_right[2],
        )
        for b in range(3):
            span = slice(b * TILE, (b + 1) * TILE)
            inverse = 1.0 / sums[b][0:1]
            delta = sums[b][1:2] * inverse
            share = (inverse * to_right[0], inverse, inverse * to_left[2])[b]
            probs = exps[slot, :, span] * share
            low[0, :, span] = probs.astype(BF16)
            low[1, :, span] = (probs * (gprobs[slot, :, span] - delta)).astype(BF16)
        give_result(2, h, product(low[0], pair[h, 1]).astype(BF16))
        grad_hat = product(low[1], pair[h, 0]) * SCALE
        k = k_raw[h].astype(F32)
        inverse = inverse_norm(k)
        give_result(1, h, norm_back(grad_hat, k, gains[seg, 1:2], inverse).astype(BF16))
        turned = product(k_turned[h], low[1])
        dq_out[h, 0] = turned[:, :TILE].astype(BF16)
        dq_out[h, 1] = turned[:, 2 * TILE :].astype(BF16)
        dq_own[h] = turned[:, TILE : 2 * TILE]
        gain_acc[seg, 0:1] += jnp.sum(grad_hat * k_hat[h].astype(F32), axis=0, keepdims=True) / gains[seg, 0:1]
        gain_acc[seg, 1:2] += jnp.sum(grad_hat * (k * inverse), axis=0, keepdims=True)

    def give_dq(h, carry):
        for side in (0, 1):
            send_dq(h, side).start()
        return carry

    def query_grads(h, carry):
        for side in (0, 1):
            send_dq(h, side).wait_recv()
        total = dq_own[h] + dq_in[h, 0].astype(F32) + dq_in[h, 1].astype(F32)
        q = q_raw[h].astype(F32)
        grad = norm_back((total * SCALE).T, q, gains[segment(h), 0:1], inverse_norm(q))
        give_result(0, h, grad.astype(BF16))
        return carry

    gain_acc[...] = jnp.zeros_like(gain_acc)
    normalize(0)
    pl.semaphore_wait(barrier, len(greeted))
    give_pair(0)
    for copy in infos:
        copy.start()
    for copy in swaps(KEPT):
        copy.start()
    lax.fori_loop(1, KEPT, start_loads, 0)
    for h in range(KEPT + 1, HEADS):
        for copy in swaps(h):
            copy.start()
    for h in range(1, AHEAD):
        normalize(h)
        give_pair(h)
    for h in range(AHEAD):
        normalize_key(h)

    def given(i):
        early = (jnp.clip(i - GRAD_LAG, 0, HEADS) * EARLY) // 6
        late = (i - DQ_FROM + 1) * RATE
        return jnp.clip(jnp.minimum(jnp.maximum(early, late), i - GRAD_LAG + 1), 0, HEADS)

    def taken(i):
        return given(i - WAIT)

    def step(i, carry):
        @pl.when(i < HEADS)
        def _():
            scores(i)

        @pl.when(i + AHEAD < HEADS)
        def _():
            normalize(i + AHEAD)
            give_pair(i + AHEAD)
            normalize_key(i + AHEAD)

        @pl.when(i == 0)
        def _():
            for copy in infos:
                copy.wait_recv()

        @pl.when(i >= GRAD_LAG)
        def _():
            grads(i - GRAD_LAG)

        lax.fori_loop(given(i - 1), given(i), give_dq, 0)
        lax.fori_loop(taken(i - 1), taken(i), query_grads, 0)
        return carry

    lax.fori_loop(0, STEPS, step, 0)
    lax.fori_loop(given(STEPS - 1), HEADS, give_dq, 0)

    def first(j, other):
        to, sender = lax.rem(d + j, dps), lax.rem(d + dps - j, dps)
        copy = remote(
            gain_acc.at[other], first_slots.at[other, d], first_send.at[other, j], first_recv.at[other, j],
            (1 - p if other else p, s, to),
        )
        arrival = remote(
            gain_acc.at[other], first_slots.at[other, sender], first_send.at[other, j], first_recv.at[other, j],
            (1 - p if other else p, s, to),
        )
        return copy, arrival

    def later(axis, j):
        mine, size, device = groups[axis]
        to, sender = device(lax.rem(mine + j, size)), lax.rem(mine + size - j, size)
        return [
            remote(
                gain_slots.at[axis, mine], gain_slots.at[axis, slot],
                gain_send.at[axis, j - 1], gain_recv.at[axis, j - 1], to,
            )
            for slot in (mine, sender)
        ]

    rounds = [[first(j, other) for other in (0, 1) for j in range(1 - other, dps)]]
    rounds += [[later(axis, j) for j in range(1, groups[axis][1])] for axis in (0, 1)]

    def begin(r, value):
        if r == 0:
            first_slots[0, d] = value
        else:
            gain_slots[r - 1, groups[r - 1][0]] = value
        for copy, _ in rounds[r]:
            copy.start()

    def end(r):
        for _, arrival in rounds[r]:
            arrival.wait_recv()
        for copy, _ in rounds[r]:
            copy.wait_send()
        if r == 0:
            slots = [first_slots[other, j] for other in (0, 1) for j in range(dps)]
        else:
            slots = [gain_slots[r - 1, j] for j in range(groups[r - 1][1])]
        total = slots[0]
        for slot in slots[1:]:
            total = total + slot
        return total

    begin(0, gain_acc[0])
    done, rest = taken(STEPS - 1), HEADS - taken(STEPS - 1)
    marks = [done, done + rest // 2, done + rest * 3 // 4, HEADS]
    for r in range(3):
        lax.fori_loop(marks[r], marks[r + 1], query_grads, 0)
        total = end(r)
        if r < 2:
            begin(r + 1, total)
        else:
            gain_out[...] = total * (1.0 / math.sqrt(dps * seqs * TILE * HEADS))

    for copy in infos:
        copy.wait_send()

    kept, swapped = pl.ds(0, KEPT * DIM), pl.ds(KEPT * DIM, SWAPPED * DIM)
    for side in (0, 1):
        own = pair.at[:, :, pl.ds(TILE, TILE)]
        remote(own, own, in_send.at[side], in_send.at[side], sides[side]).wait_send()
        own = dq_out.at[:, side]
        remote(own, own, dq_send.at[side], dq_send.at[side], sides[side]).wait_send()
    for e, own in enumerate(
        (stat.at[:, pl.ds(0, 2)], stat.at[:, pl.ds(1, 2)], stat.at[:, pl.ds(0, 1)], stat.at[:, pl.ds(2, 1)])
    ):
        remote(own, own, stat_send.at[e], stat_send.at[e], left).wait_send()
    for part, source in enumerate((q_ref, k_ref, g_ref, v_ref)):
        own = source.at[:, swapped]
        remote(own, own, swap_send.at[part], swap_send.at[part], across).wait_send()
    final = remote(results, out_ref.at[:, :, kept], out_send.at[0], out_recv.at[0], across)
    final.wait_send()
    final.wait_recv()


def solution(mesh):
    seqs, dps = mesh.shape["seq"], mesh.shape["dp"]
    zs = 4
    dma, vmem = pltpu.SemaphoreType.DMA, pltpu.VMEM

    def body(*refs):
        kernel(seqs, dps, zs, *refs)

    call = pl.pallas_call(
        body,
        out_shape=(
            pltpu.VMEM((3, TILE, HEADS * DIM), BF16),
            jax.ShapeDtypeStruct((2, DIM), F32),
        ),
        in_specs=[pl.BlockSpec(memory_space=pl.ANY)] * 4
        + [pl.BlockSpec(memory_space=pltpu.VMEM), pl.BlockSpec(memory_space=pltpu.SMEM)],
        out_specs=(pl.BlockSpec(memory_space=pltpu.VMEM), pl.BlockSpec(memory_space=pltpu.VMEM)),
        scratch_shapes=[
            vmem((HEADS, TILE, DIM), BF16),
            vmem((HEADS, TILE, DIM), BF16),
            vmem((HEADS, TILE, DIM), BF16),
            vmem((HEADS, 2, SPAN, DIM), BF16),
            vmem((HEADS, TILE, DIM), BF16),
            vmem((HEADS, DIM, TILE), BF16),
            vmem((SLOTS, TILE, SPAN), F32),
            vmem((SLOTS, TILE, SPAN), F32),
            vmem((2, TILE, SPAN), BF16),
            vmem((HEADS, 3, 2, TILE), F32),
            vmem((HEADS, 2, 2, TILE), F32),
            vmem((HEADS, 2, 2, TILE), F32),
            vmem((HEADS, 1, 2, TILE), F32),
            vmem((HEADS, 1, 2, TILE), F32),
            vmem((2, 3, 2, TILE), F32),
            vmem((2, 2, DIM), F32),
            vmem((HEADS, DIM, TILE), F32),
            vmem((HEADS, 2, DIM, TILE), BF16),
            vmem((HEADS, 2, DIM, TILE), BF16),
            vmem((3, KEPT, TILE, DIM), BF16),
            vmem((2, 2, DIM), F32),
            vmem((2, dps, 2, DIM), F32),
            vmem((2, 4, 2, DIM), F32),
            dma((4, HEADS)),
            dma((4,)),
            dma((4, SWAPPED)),
            dma((2,)),
            dma((HEADS, 2)),
            dma((4,)),
            dma((HEADS, 4)),
            dma((6,)),
            dma((6,)),
            dma((2,)),
            dma((HEADS, 2)),
            dma((1,)),
            dma((1,)),
            dma((2, dps)),
            dma((2, dps)),
            dma((2, 3)),
            dma((2, 3)),
        ],
        compiler_params=pltpu.CompilerParams(
            collective_id=0, has_side_effects=True, vmem_limit_bytes=58 * 2**20
        ),
        cost_estimate=pl.CostEstimate(
            flops=10 * TILE * SPAN * HEADS * DIM,
            bytes_accessed=7 * 2 * TILE * HEADS * DIM,
            transcendentals=TILE * SPAN * HEADS,
        ),
    )

    def local(queries, keys, values, grad_out, norm_gains, kv_tiles):
        grads, gain_grads = call(
            queries[0, 0, 0], keys[0, 0, 0], values[0, 0, 0], grad_out[0, 0, 0],
            norm_gains[0], kv_tiles[0, 0],
        )
        return grads[None, :, None, None], gain_grads[None]

    tokens = P("pipe", "dp", "seq", None, None)
    return jax.shard_map(
        local,
        mesh=mesh,
        in_specs=(tokens,) * 4 + (P("pipe", None, None), P("pipe", "dp", "seq", None)),
        out_specs=(P("pipe", None, "dp", "seq", None, None), P("pipe", None, None)),
        check_vma=False,
    )
```

```python
import math

import jax
import jax.numpy as jnp
from jax import lax
from jax.experimental import pallas as pl
from jax.experimental.pallas import tpu as pltpu
from jax.sharding import PartitionSpec as P

HEADS = 12
DIM = 128
TILE = 384
SPAN = 3 * TILE
EPSILON = 1e-06
SCALE = DIM**-0.5
EXP2_SCALE = SCALE * math.log2(math.e)
MESH = pl.DeviceIdType.MESH
BF16, F32 = jnp.bfloat16, jnp.float32

SWAPPED = 3
KEPT = HEADS - SWAPPED
GRAD_LAG, AHEAD, DQ_FROM, RATE, EARLY, WAIT = 2, 3, 9, 2, 1, 3
SLOTS = GRAD_LAG + 1
STEPS = HEADS + GRAD_LAG


def over_rows(a, b):
    return lax.dot_general(a, b, (((1,), (1,)), ((), ())), preferred_element_type=F32)


def product(a, b):
    return lax.dot_general(a, b, (((1,), (0,)), ((), ())), preferred_element_type=F32)


def inverse_norm(x):
    return lax.rsqrt(jnp.mean(x * x, axis=-1, keepdims=True) + EPSILON)


def norm_back(grad_hat, x, gain, inverse):
    projected = jnp.sum(gain * grad_hat * x, axis=-1, keepdims=True)
    return inverse * (gain * grad_hat) - x * (inverse * inverse * inverse * projected * (1.0 / DIM))


def kernel(
    seqs, dps, zs,
    q_ref, k_ref, v_ref, g_ref, gain_ref, list_ref,
    out_ref, gain_out,
    q_raw, k_raw, v_in, pair, k_hat, k_turned, exps, gprobs, low,
    stat, stat_l, stat_r, stat_ll, stat_rr, masks, gains,
    dq_own, dq_out, dq_in, results, gain_acc, first_slots, gain_slots,
    load_sem, swap_send, swap_recv, in_send, in_recv, stat_send, stat_recv, info_send, info_recv, dq_send, dq_recv,
    out_send, out_recv, first_send, first_recv, gain_send, gain_recv,
):
    p, s, d = lax.axis_index("pipe"), lax.axis_index("seq"), lax.axis_index("dp")

    def at(q, step):
        return (q, lax.rem(s + seqs + step, seqs), d)

    left, right = at(p, -1), at(p, 1)
    sides = (left, right)
    across = at(1 - p, 0)
    xs = seqs // zs
    x, z = s // zs, lax.rem(s, zs)
    groups = (
        (x, xs, lambda i: (p, i * zs + z, d)),
        (z, zs, lambda i: (p, x * zs + i, d)),
    )

    def columns(h):
        return pl.ds(pl.multiple_of(h * DIM, DIM), DIM)

    def remote(source, target, send, recv, device):
        return pltpu.make_async_remote_copy(
            src_ref=source, dst_ref=target, send_sem=send, recv_sem=recv,
            device_id=device, device_id_type=MESH,
        )

    def places(h):
        return (
            (q_ref, q_raw.at[h]),
            (k_ref, k_raw.at[h]),
            (g_ref, pair.at[h, 1, pl.ds(TILE, TILE)]),
            (v_ref, v_in.at[h]),
        )

    def loads(h):
        return [
            pltpu.make_async_copy(source.at[:, columns(h)], target, load_sem.at[part, h])
            for part, (source, target) in enumerate(places(h))
        ]

    def swaps(h):
        return [
            remote(
                source.at[:, columns(h)], target,
                swap_send.at[part], swap_recv.at[part, h - KEPT], across,
            )
            for part, (source, target) in enumerate(places(h))
        ]

    def start_loads(h, carry):
        for copy in loads(h):
            copy.start()
        return carry

    lax.fori_loop(0, KEPT, start_loads, 0)

    barrier = pltpu.get_barrier_semaphore()
    greeted = [at(p, -1), at(p, 1), at(p, -2), at(p, 2), at(1 - p, -1), at(1 - p, 0), at(1 - p, 1)]
    for j in range(1, dps):
        greeted += [(q, s, lax.rem(d + j, dps)) for q in (p, 1 - p)]
    for mine, size, device in groups:
        greeted += [device(lax.rem(mine + j, size)) for j in range(1, size)]
    for device in greeted:
        pl.semaphore_signal(barrier, inc=1, device_id=device, device_id_type=MESH)

    def names(tile):
        named = (list_ref[0, 0] == tile) | (list_ref[0, 1] == tile) | (list_ref[0, 2] == tile)
        return jnp.where(named, 1.0, 0.0).astype(F32)

    masks[0, 1, 0:1] = jnp.full((1, TILE), jnp.where(s > 0, names(s - 1), 0.0), F32)
    masks[0, 1, 1:2] = jnp.full((1, TILE), names(s + 1), F32)
    gains[0] = gain_ref[...]

    own_masks = masks.at[0, 1]
    infos = [
        remote(own_masks, masks.at[q, t], info_send.at[e], info_recv.at[e], device)
        for e, (q, t, device) in enumerate(
            (
                (0, 2, at(p, -1)), (0, 0, at(p, 1)),
                (1, 2, at(1 - p, -1)), (1, 0, at(1 - p, 1)), (1, 1, across),
            )
        )
    ]
    infos.append(remote(gains.at[0], gains.at[1], info_send.at[5], info_recv.at[5], across))

    def send_pair(h, side):
        return remote(
            pair.at[h, :, pl.ds(TILE, TILE)], pair.at[h, :, pl.ds(2 * TILE * (1 - side), TILE)],
            in_send.at[side], in_recv.at[h, 1 - side], sides[side],
        )

    def send_dq(h, side):
        return remote(
            dq_out.at[h, side], dq_in.at[h, 1 - side], dq_send.at[side], dq_recv.at[h, 1 - side], sides[side]
        )

    def send_stats(h):
        return [
            remote(source, target.at[h], stat_send.at[e], stat_recv.at[h, e], device)
            for e, (source, target, device) in enumerate(
                (
                    (stat.at[h, pl.ds(0, 2)], stat_r, left),
                    (stat.at[h, pl.ds(1, 2)], stat_l, right),
                    (stat.at[h, pl.ds(0, 1)], stat_rr, at(p, -2)),
                    (stat.at[h, pl.ds(2, 1)], stat_ll, at(p, 2)),
                )
            )
        ]

    def send_result(part, h):
        return remote(
            results.at[part, h], out_ref.at[part, :, columns(h)],
            out_send.at[0], out_recv.at[0], across,
        )

    def give_result(part, h, value):
        @pl.when(h < KEPT)
        def _():
            results[part, h] = value
            send_result(part, h).start()

        @pl.when(h >= KEPT)
        def _():
            out_ref[part, :, columns(h)] = value

    def segment(h):
        return jnp.where(h >= KEPT, 1, 0)

    def normalize(h):
        @pl.when(h < KEPT)
        def _():
            for copy in loads(h):
                copy.wait()

        @pl.when(h >= KEPT)
        def _():
            for copy in swaps(h):
                copy.wait_recv()

        q = q_raw[h].astype(F32)
        pair[h, 0, TILE : 2 * TILE] = (q * inverse_norm(q) * gains[segment(h), 0:1]).astype(BF16)

    def normalize_key(h):
        k = k_raw[h].astype(F32)
        hat = k * inverse_norm(k) * gains[segment(h), 1:2]
        k_hat[h] = hat.astype(BF16)
        k_turned[h] = hat.T.astype(BF16)

    def give_pair(h):
        for side in (0, 1):
            send_pair(h, side).start()

    def scores(h):
        for side in (0, 1):
            send_pair(h, side).wait_recv()
        slot = lax.rem(h, SLOTS)
        for b in range(3):
            span = slice(b * TILE, (b + 1) * TILE)
            e = jnp.exp2(over_rows(k_hat[h], pair[h, 0, span]) * EXP2_SCALE)
            g = over_rows(v_in[h], pair[h, 1, span])
            exps[slot, :, span] = e
            gprobs[slot, :, span] = g
            stat[h, b, 0:1] = jnp.sum(e, axis=0, keepdims=True)
            stat[h, b, 1:2] = jnp.sum(e * g, axis=0, keepdims=True)
        for copy in send_stats(h):
            copy.start()

    def grads(h):
        for copy in send_stats(h):
            copy.wait_recv()
        slot, seg = lax.rem(h, SLOTS), segment(h)
        to_left = [masks[seg, t, 0:1] for t in range(3)]
        to_right = [masks[seg, t, 1:2] for t in range(3)]
        sums = (
            stat[h, 0] * to_right[0] + stat_l[h, 0] + stat_ll[h, 0] * to_left[0],
            stat[h, 1] + stat_l[h, 1] * to_left[1] + stat_r[h, 0] * to_right[1],
            stat[h, 2] * to_left[2] + stat_r[h, 1] + stat_rr[h, 0] * to_right[2],
        )
        for b in range(3):
            span = slice(b * TILE, (b + 1) * TILE)
            inverse = 1.0 / sums[b][0:1]
            delta = sums[b][1:2] * inverse
            share = (inverse * to_right[0], inverse, inverse * to_left[2])[b]
            probs = exps[slot, :, span] * share
            low[0, :, span] = probs.astype(BF16)
            low[1, :, span] = (probs * (gprobs[slot, :, span] - delta)).astype(BF16)
        give_result(2, h, product(low[0], pair[h, 1]).astype(BF16))
        grad_hat = product(low[1], pair[h, 0]) * SCALE
        k = k_raw[h].astype(F32)
        inverse = inverse_norm(k)
        give_result(1, h, norm_back(grad_hat, k, gains[seg, 1:2], inverse).astype(BF16))
        turned = product(k_turned[h], low[1])
        dq_out[h, 0] = turned[:, :TILE].astype(BF16)
        dq_out[h, 1] = turned[:, 2 * TILE :].astype(BF16)
        dq_own[h] = turned[:, TILE : 2 * TILE]
        gain_acc[seg, 0:1] += jnp.sum(grad_hat * k_hat[h].astype(F32), axis=0, keepdims=True) / gains[seg, 0:1]
        gain_acc[seg, 1:2] += jnp.sum(grad_hat * (k * inverse), axis=0, keepdims=True)

    def give_dq(h, carry):
        for side in (0, 1):
            send_dq(h, side).start()
        return carry

    def query_grads(h, carry):
        for side in (0, 1):
            send_dq(h, side).wait_recv()
        total = dq_own[h] + dq_in[h, 0].astype(F32) + dq_in[h, 1].astype(F32)
        q = q_raw[h].astype(F32)
        grad = norm_back((total * SCALE).T, q, gains[segment(h), 0:1], inverse_norm(q))
        give_result(0, h, grad.astype(BF16))
        return carry

    gain_acc[...] = jnp.zeros_like(gain_acc)
    normalize(0)
    pl.semaphore_wait(barrier, len(greeted))
    give_pair(0)
    for copy in infos:
        copy.start()
    for h in range(KEPT, HEADS):
        for copy in swaps(h):
            copy.start()
    for h in range(1, AHEAD):
        normalize(h)
        give_pair(h)
    for h in range(AHEAD):
        normalize_key(h)

    def given(i):
        early = (jnp.clip(i - GRAD_LAG, 0, HEADS) * EARLY) // 6
        late = (i - DQ_FROM + 1) * RATE
        return jnp.clip(jnp.minimum(jnp.maximum(early, late), i - GRAD_LAG + 1), 0, HEADS)

    def taken(i):
        return given(i - WAIT)

    def step(i, carry):
        @pl.when(i < HEADS)
        def _():
            scores(i)

        @pl.when(i + AHEAD < HEADS)
        def _():
            normalize(i + AHEAD)
            give_pair(i + AHEAD)
            normalize_key(i + AHEAD)

        @pl.when(i == 0)
        def _():
            for copy in infos:
                copy.wait_recv()

        @pl.when(i >= GRAD_LAG)
        def _():
            grads(i - GRAD_LAG)

        lax.fori_loop(given(i - 1), given(i), give_dq, 0)
        lax.fori_loop(taken(i - 1), taken(i), query_grads, 0)
        return carry

    lax.fori_loop(0, STEPS, step, 0)
    lax.fori_loop(given(STEPS - 1), HEADS, give_dq, 0)

    def first(j, other):
        to, sender = lax.rem(d + j, dps), lax.rem(d + dps - j, dps)
        copy = remote(
            gain_acc.at[other], first_slots.at[other, d], first_send.at[other, j], first_recv.at[other, j],
            (1 - p if other else p, s, to),
        )
        arrival = remote(
            gain_acc.at[other], first_slots.at[other, sender], first_send.at[other, j], first_recv.at[other, j],
            (1 - p if other else p, s, to),
        )
        return copy, arrival

    def later(axis, j):
        mine, size, device = groups[axis]
        to, sender = device(lax.rem(mine + j, size)), lax.rem(mine + size - j, size)
        return [
            remote(
                gain_slots.at[axis, mine], gain_slots.at[axis, slot],
                gain_send.at[axis, j - 1], gain_recv.at[axis, j - 1], to,
            )
            for slot in (mine, sender)
        ]

    rounds = [[first(j, other) for other in (0, 1) for j in range(1 - other, dps)]]
    rounds += [[later(axis, j) for j in range(1, groups[axis][1])] for axis in (0, 1)]

    def begin(r, value):
        if r == 0:
            first_slots[0, d] = value
        else:
            gain_slots[r - 1, groups[r - 1][0]] = value
        for copy, _ in rounds[r]:
            copy.start()

    def end(r):
        for _, arrival in rounds[r]:
            arrival.wait_recv()
        for copy, _ in rounds[r]:
            copy.wait_send()
        if r == 0:
            slots = [first_slots[other, j] for other in (0, 1) for j in range(dps)]
        else:
            slots = [gain_slots[r - 1, j] for j in range(groups[r - 1][1])]
        total = slots[0]
        for slot in slots[1:]:
            total = total + slot
        return total

    begin(0, gain_acc[0])
    done, rest = taken(STEPS - 1), HEADS - taken(STEPS - 1)
    marks = [done, done + rest // 2, done + rest * 3 // 4, HEADS]
    for r in range(3):
        lax.fori_loop(marks[r], marks[r + 1], query_grads, 0)
        total = end(r)
        if r < 2:
            begin(r + 1, total)
        else:
            gain_out[...] = total * (1.0 / math.sqrt(dps * seqs * TILE * HEADS))

    for copy in infos:
        copy.wait_send()

    kept, swapped = pl.ds(0, KEPT * DIM), pl.ds(KEPT * DIM, SWAPPED * DIM)
    for side in (0, 1):
        own = pair.at[:, :, pl.ds(TILE, TILE)]
        remote(own, own, in_send.at[side], in_send.at[side], sides[side]).wait_send()
        own = dq_out.at[:, side]
        remote(own, own, dq_send.at[side], dq_send.at[side], sides[side]).wait_send()
    for e, own in enumerate(
        (stat.at[:, pl.ds(0, 2)], stat.at[:, pl.ds(1, 2)], stat.at[:, pl.ds(0, 1)], stat.at[:, pl.ds(2, 1)])
    ):
        remote(own, own, stat_send.at[e], stat_send.at[e], left).wait_send()
    for part, source in enumerate((q_ref, k_ref, g_ref, v_ref)):
        own = source.at[:, swapped]
        remote(own, own, swap_send.at[part], swap_send.at[part], across).wait_send()
    final = remote(results, out_ref.at[:, :, kept], out_send.at[0], out_recv.at[0], across)
    final.wait_send()
    final.wait_recv()


def solution(mesh):
    seqs, dps = mesh.shape["seq"], mesh.shape["dp"]
    zs = 4
    dma, vmem = pltpu.SemaphoreType.DMA, pltpu.VMEM

    def body(*refs):
        kernel(seqs, dps, zs, *refs)

    call = pl.pallas_call(
        body,
        out_shape=(
            pltpu.VMEM((3, TILE, HEADS * DIM), BF16),
            jax.ShapeDtypeStruct((2, DIM), F32),
        ),
        in_specs=[pl.BlockSpec(memory_space=pl.ANY)] * 4
        + [pl.BlockSpec(memory_space=pltpu.VMEM), pl.BlockSpec(memory_space=pltpu.SMEM)],
        out_specs=(pl.BlockSpec(memory_space=pltpu.VMEM), pl.BlockSpec(memory_space=pltpu.VMEM)),
        scratch_shapes=[
            vmem((HEADS, TILE, DIM), BF16),
            vmem((HEADS, TILE, DIM), BF16),
            vmem((HEADS, TILE, DIM), BF16),
            vmem((HEADS, 2, SPAN, DIM), BF16),
            vmem((HEADS, TILE, DIM), BF16),
            vmem((HEADS, DIM, TILE), BF16),
            vmem((SLOTS, TILE, SPAN), F32),
            vmem((SLOTS, TILE, SPAN), F32),
            vmem((2, TILE, SPAN), BF16),
            vmem((HEADS, 3, 2, TILE), F32),
            vmem((HEADS, 2, 2, TILE), F32),
            vmem((HEADS, 2, 2, TILE), F32),
            vmem((HEADS, 1, 2, TILE), F32),
            vmem((HEADS, 1, 2, TILE), F32),
            vmem((2, 3, 2, TILE), F32),
            vmem((2, 2, DIM), F32),
            vmem((HEADS, DIM, TILE), F32),
            vmem((HEADS, 2, DIM, TILE), BF16),
            vmem((HEADS, 2, DIM, TILE), BF16),
            vmem((3, KEPT, TILE, DIM), BF16),
            vmem((2, 2, DIM), F32),
            vmem((2, dps, 2, DIM), F32),
            vmem((2, 4, 2, DIM), F32),
            dma((4, HEADS)),
            dma((4,)),
            dma((4, SWAPPED)),
            dma((2,)),
            dma((HEADS, 2)),
            dma((4,)),
            dma((HEADS, 4)),
            dma((6,)),
            dma((6,)),
            dma((2,)),
            dma((HEADS, 2)),
            dma((1,)),
            dma((1,)),
            dma((2, dps)),
            dma((2, dps)),
            dma((2, 3)),
            dma((2, 3)),
        ],
        compiler_params=pltpu.CompilerParams(
            collective_id=0, has_side_effects=True, vmem_limit_bytes=58 * 2**20
        ),
        cost_estimate=pl.CostEstimate(
            flops=10 * TILE * SPAN * HEADS * DIM,
            bytes_accessed=7 * 2 * TILE * HEADS * DIM,
            transcendentals=TILE * SPAN * HEADS,
        ),
    )

    def local(queries, keys, values, grad_out, norm_gains, kv_tiles):
        grads, gain_grads = call(
            queries[0, 0, 0], keys[0, 0, 0], values[0, 0, 0], grad_out[0, 0, 0],
            norm_gains[0], kv_tiles[0, 0],
        )
        return grads[None, :, None, None], gain_grads[None]

    tokens = P("pipe", "dp", "seq", None, None)
    return jax.shard_map(
        local,
        mesh=mesh,
        in_specs=(tokens,) * 4 + (P("pipe", None, None), P("pipe", "dp", "seq", None)),
        out_specs=(P("pipe", None, "dp", "seq", None, None), P("pipe", None, None)),
        check_vma=False,
    )
```
